32 devices in a mesh: orb: 2 (over core), box: 16 (over z, y, x).
Axes of the slice: x: 2, y: 2, z: 4, core: 2. Of those that a mesh axis runs over, the one named last changes fastest.
Arguments:
- orbitals: bfloat16 [768, 128, 1000], P('orb', 'box'), may hold values from -6 to 6
- exchange_values: bfloat16 [768, 128, 1000], P('orb', 'box'), may hold values from -6 to 6
- local_values: float32 [128, 1000], P('box'), may hold values from -6 to 6
- coupling: bfloat16 [768, 768], P('orb'), may hold values from -0.21875 to 0.21875
- to_values_mat: float32 [10, 10], replicated, may hold values from -2 to 2
- to_coeffs_mat: float32 [10, 10], replicated, may hold values from -2 to 2
- laplace_blocks: float32 [3, 10, 10], replicated, may hold values from -2 to 2
- box_counts: int32 [16], P('box'), may hold values from 2 to 8, as said below
- kept_mask: int32 [128], P('box'), may hold values from 0 to 1, as said below
- send_list: int32 [16, 16], P('box'), may hold values from -1 to 7, as said below
- neighbour_pos: int32 [6, 128], P(None, 'box'), may hold values from -1 to 23, as said below
Outputs:
- h_orbitals: bfloat16 [768, 128, 1000], P('orb', 'box')
The draws below stay inside these ranges and needn't reach their ends.
Inputs may be any that keep to these rules, and one draw needn't show every extreme that they name: Device d of box holds live boxes in slots 0 to box_counts[d] - 1 of its 8; some device holds 8. `kept_mask`: 1 only on live boxes; at most 4 ones in one device's range, and exactly 4 in some device's range. `send_list`: row q, entries p * 1 to p + 1 - 1: live slots of device q's range passed to device p, -1 for an empty entry; nothing to its own device; at most 1 to one device, exactly 1 to the devices whose index differs by one. `neighbour_pos`: -1: no neighbour; below 8: a live slot of the same device; otherwise the entry of send_list named in the reference program, which is never -1. Boxes that are not live have -1 on every face.
All inputs are finite; a program needn't handle non-finite values.
Results may differ from the reference program's by a relative error of at most 0.0031.
Values may be sent and summed in bfloat16 or wider, within the bound.
A program may use at most 320 MiB of HBM per device.

```python
import jax
import jax.numpy as jnp
from jax import lax

K = 10
COEF = 1000
ORBITALS = 768
ORB_DEV = 384
BOX_DEV = 8
BOXES = 128
CAP = 1
KEEP = 4
N_BOX = 16


def build_layout(key):
    keys = jax.random.split(jax.random.fold_in(key, 11), 9)
    devices = BOXES // BOX_DEV
    dev_ids = jnp.arange(devices, dtype=jnp.int32)
    counts = jax.random.randint(keys[0], (devices,), BOX_DEV // 4, BOX_DEV + 1)
    fullest = jax.random.randint(keys[1], (), 0, devices)
    counts = jnp.where(dev_ids == fullest, BOX_DEV, counts).astype(jnp.int32)
    spread = jax.random.randint(keys[2], (devices, devices), 0, CAP + 1)
    distance = jnp.abs(dev_ids[:, None] - dev_ids[None, :])
    sent = jnp.where(distance == 1, CAP, spread)
    sent = jnp.where(distance == 0, 0, sent)
    positions = jnp.arange(CAP, dtype=jnp.int32)
    used = positions[None, None, :] < sent[:, :, None]
    chosen = jax.random.randint(keys[3], (devices, devices, CAP), 0, BOX_DEV) % counts[:, None, None]
    send_list = jnp.where(used, chosen, -1).reshape(devices, devices * CAP).astype(jnp.int32)
    arrive = jnp.transpose(used, (1, 0, 2)).reshape(devices, devices * CAP).astype(jnp.int32)
    arrived = jnp.sum(arrive, axis=1)
    running = jnp.cumsum(arrive, axis=1)
    kinds = jax.random.randint(keys[4], (6, devices, BOX_DEV), 0, 10)
    local_pick = jax.random.randint(keys[5], (6, devices, BOX_DEV), 0, BOX_DEV) % counts[None, :, None]
    ranks = jax.random.randint(keys[6], (6, devices, BOX_DEV), 0, 1 << 20) % arrived[None, :, None]
    remote_pick = jnp.sum((running[None, :, None, :] <= ranks[..., None]).astype(jnp.int32), axis=-1)
    faces = jnp.where(kinds == 0, -1, jnp.where(kinds <= 2, local_pick, BOX_DEV + remote_pick))
    slot_ids = jnp.arange(BOX_DEV, dtype=jnp.int32)
    live = slot_ids[None, :] < counts[:, None]
    faces = jnp.where(live[None, :, :], faces, -1).reshape(6, devices * BOX_DEV).astype(jnp.int32)
    quota = jnp.minimum(counts, jax.random.randint(keys[7], (devices,), KEEP // 4, KEEP + 1))
    quota = jnp.where(dev_ids == fullest, KEEP, quota)
    scores = jax.random.randint(keys[8], (devices, BOX_DEV), 0, 1 << 16) * BOX_DEV + slot_ids[None, :]
    scores = jnp.where(live, scores, (1 << 16) * BOX_DEV + slot_ids[None, :])
    order = jnp.argsort(scores, axis=1)
    place = jnp.argsort(order, axis=1)
    kept = (place < quota[:, None]).astype(jnp.int32).reshape(devices * BOX_DEV)
    return (counts, kept, send_list, faces)


def draw_box_counts(key, part):
    return build_layout(key)[0]


def draw_kept_mask(key, part):
    return build_layout(key)[1]


def draw_send_list(key, part):
    return build_layout(key)[2]


def draw_neighbour_pos(key, part):
    return build_layout(key)[3]


def steps_of(own_key, dims, cuts, low, top_value):
    def one(dim, parts):
        steps = jax.random.uniform(jax.random.fold_in(jax.random.fold_in(own_key, 6), dim), (parts,), jnp.float32, low / len(cuts), top_value / len(cuts))
        return jnp.repeat(jnp.exp(steps), dims[dim] // parts).reshape((-1,) + (1,) * (len(dims) - dim - 1))

    level = one(*cuts[0])
    for cut in cuts[1:]:
        level = level * one(*cut)
    return level


def bell_draw(own_key, shape, scale, reach, cuts=(), kind=jnp.bfloat16):
    values = jax.random.normal(own_key, shape, jnp.float32) * scale
    if len(cuts) > 0:
        values = steps_of(own_key, shape, cuts, -0.22, 0.18) * values
    return jnp.clip(values, min=-reach, max=reach).astype(kind)


def setup_inputs(seed: int = 0) -> dict:
    arg_keys = jax.random.split(jax.random.key(seed), 12)
    return {
        "orbitals": bell_draw(arg_keys[0], (ORBITALS, BOXES, COEF), 1.0, 6.0, ((0, 2), (1, 16))),
        "exchange_values": bell_draw(arg_keys[1], (ORBITALS, BOXES, COEF), 1.0, 6.0, ((0, 2), (1, 16))),
        "local_values": bell_draw(arg_keys[2], (BOXES, COEF), 1.0, 6.0, ((0, 16),), jnp.float32),
        "coupling": bell_draw(arg_keys[3], (ORBITALS, ORBITALS), ORBITALS ** -0.5, 0.21875, ((0, 2),)),
        "to_values_mat": bell_draw(arg_keys[4], (K, K), K ** -0.5, 2.0, (), jnp.float32),
        "to_coeffs_mat": bell_draw(arg_keys[5], (K, K), K ** -0.5, 2.0, (), jnp.float32),
        "laplace_blocks": bell_draw(arg_keys[6], (3, K, K), K ** -0.5, 2.0, (), jnp.float32),
        "box_counts": draw_box_counts(jax.random.fold_in(arg_keys[11], 71), 0),
        "kept_mask": draw_kept_mask(jax.random.fold_in(arg_keys[11], 71), 0),
        "send_list": draw_send_list(jax.random.fold_in(arg_keys[11], 71), 0),
        "neighbour_pos": draw_neighbour_pos(jax.random.fold_in(arg_keys[11], 71), 0),
    }


def along_axis(field, matrix, which):
    forms = ("ax,nxbc->nabc", "bx,naxc->nabc", "cx,nabx->nabc")
    return jnp.einsum(forms[which], matrix, field, precision=lax.Precision.HIGHEST)


def three_way(field, matrix):
    result = along_axis(field, matrix, 0)
    result = along_axis(result, matrix, 1)
    return along_axis(result, matrix, 2)


def neighbour_index(send_list, neighbour_pos):
    boxes_all = neighbour_pos.shape[1]
    owner = (jnp.arange(boxes_all, dtype=jnp.int32) // BOX_DEV)[None, :]
    remote = neighbour_pos - BOX_DEV
    source = jnp.clip(remote // CAP, 0, N_BOX - 1).astype(jnp.int32)
    within = (jnp.maximum(remote, 0) % CAP).astype(jnp.int32)
    column = (owner * CAP + within).astype(jnp.int32)
    slot = send_list[source, column]
    remote_global = source * BOX_DEV + slot
    local_global = owner * BOX_DEV + neighbour_pos
    chosen = jnp.where(neighbour_pos < BOX_DEV, local_global, remote_global)
    return jnp.where(neighbour_pos < 0, -1, chosen).astype(jnp.int32)


def reference(orbitals, exchange_values, local_values, coupling, to_values_mat, to_coeffs_mat, laplace_blocks, box_counts, kept_mask, send_list, neighbour_pos):
    global_index = neighbour_index(send_list, neighbour_pos)
    present = global_index >= 0
    safe_index = jnp.maximum(global_index, 0).astype(jnp.int32)
    slot_of = jnp.arange(BOXES, dtype=jnp.int32) % BOX_DEV
    live = slot_of < jnp.repeat(box_counts, BOX_DEV)
    kept = kept_mask > 0
    groups = ORBITALS // ORB_DEV
    cells = (-1, K, K, K)

    def to_values(block):
        shaped = block.astype(jnp.float32).reshape(cells)
        return three_way(shaped, to_values_mat).reshape(block.shape)

    def product_block(pair):
        block, potential = pair
        values = to_values(block)
        weighted = jnp.where(kept[None, :, None], potential.astype(jnp.float32) * values, jnp.float32(0.0))
        return weighted.astype(jnp.bfloat16)

    orbital_blocks = orbitals.reshape(groups, ORB_DEV, BOXES, COEF)
    potential_blocks = exchange_values.reshape(groups, ORB_DEV, BOXES, COEF)
    products = lax.map(product_block, (orbital_blocks, potential_blocks))
    flat_products = products.reshape(ORBITALS, BOXES * COEF)
    coupling_blocks = coupling.reshape(groups, ORB_DEV, ORBITALS)

    def apply_block(pair):
        block, rows = pair
        values = to_values(block)
        exchange = jnp.dot(rows, flat_products, preferred_element_type=jnp.float32).reshape(ORB_DEV, BOXES, COEF)
        weighted = local_values[None, :, :] * values - exchange
        potential_part = three_way(weighted.reshape(cells), to_coeffs_mat)
        center = block.astype(jnp.float32).reshape(cells)
        kinetic = jnp.zeros_like(center)
        for which in range(3):
            kinetic = kinetic + along_axis(center, laplace_blocks[0], which)
            for side in range(2):
                face = 2 * which + side
                moved = jnp.take(block, safe_index[face], axis=1)
                moved = jnp.where(present[face][None, :, None], moved, jnp.zeros_like(moved))
                moved = moved.astype(jnp.float32).reshape(cells)
                kinetic = kinetic + along_axis(moved, laplace_blocks[1 + side], which)
        total = (potential_part - 0.5 * kinetic).reshape(ORB_DEV, BOXES, COEF)
        total = jnp.where(live[None, :, None], total, jnp.float32(0.0))
        return total.astype(jnp.bfloat16)

    result = lax.map(apply_block, (orbital_blocks, coupling_blocks))
    return result.reshape(ORBITALS, BOXES, COEF)
```

```python
import functools

import jax
import jax.numpy as jnp
from jax import lax
from jax.experimental import pallas as pl
from jax.experimental.pallas import tpu as pltpu
from jax.sharding import PartitionSpec as P

F32, BF16 = jnp.float32, jnp.bfloat16


def split(matrix):
    high = lax.reduce_precision(matrix, 8, 7)
    return high.astype(BF16), (matrix - high).astype(BF16)


def pack_kernel(slots, pool, out, sems):
    def copy(p):
        slot = jnp.maximum(slots[p], 0)
        return pltpu.make_async_copy(pool.at[slot], out.at[p], sems.at[p])

    @pl.loop(0, out.shape[0])
    def _(p):
        copy(p).start()

    @pl.loop(0, out.shape[0])
    def _(p):
        copy(p).wait()


def pack(slots, pool):
    count = slots.shape[0]
    return pl.pallas_call(
        pack_kernel,
        out_shape=jax.ShapeDtypeStruct((count,) + pool.shape[1:], pool.dtype),
        grid_spec=pltpu.PrefetchScalarGridSpec(
            num_scalar_prefetch=1,
            grid=(1,),
            in_specs=[pl.BlockSpec(memory_space=pl.ANY)],
            out_specs=pl.BlockSpec(memory_space=pl.ANY),
            scratch_shapes=[pltpu.SemaphoreType.DMA((count,))],
        ),
    )(slots, pool)


def faces_kernel(faces, count, own, come, part, far, near, out, pool, acc, sems):
    box_dev = own.shape[0]
    total = box_dev + come.shape[0]
    g = pl.program_id(0)

    def copy(n, ref, at):
        return pltpu.make_async_copy(ref.at[n], pool.at[at + n], sems.at[at + n])

    @pl.when(g == 0)
    def _():
        @pl.loop(0, box_dev)
        def _(n):
            copy(n, own, 0).start()

        @pl.loop(0, total - box_dev)
        def _(n):
            copy(n, come, box_dev).start()

        @pl.loop(0, box_dev)
        def _(n):
            copy(n, own, 0).wait()

        @pl.loop(0, total - box_dev)
        def _(n):
            copy(n, come, box_dev).wait()

    @pl.when(g >= count[0])
    def _():
        out[...] = jnp.zeros_like(out)

    @pl.when(g < count[0])
    def _():
        acc[...] = part[0]
        for f in range(6):
            at = faces[f, g]

            @pl.when(at >= 0)
            def _(f=f, at=at):
                x = pool[jnp.maximum(at, 0)]
                if f < 2:
                    acc[...] += jnp.dot(far[f, 0], x, preferred_element_type=F32) + jnp.dot(
                        far[f, 1], x, preferred_element_type=F32
                    )
                else:
                    size = near.shape[-1]
                    for j in range(x.shape[0] // size):
                        rows = pl.ds(j * size, size)
                        y = x[j * size : (j + 1) * size]
                        acc[rows, :] += jnp.dot(
                            near[f - 2, 0], y, preferred_element_type=F32
                        ) + jnp.dot(near[f - 2, 1], y, preferred_element_type=F32)

        out[0] = acc[...].astype(out.dtype)


def apply_faces(faces, count, own, come, part, far, near):
    boxes, width, orbs = own.shape
    total = boxes + come.shape[0]
    full = lambda a: pl.BlockSpec(a.shape, lambda g, *_: (0,) * a.ndim)
    block = pl.BlockSpec((1, width, orbs), lambda g, *_: (g, 0, 0))
    return pl.pallas_call(
        faces_kernel,
        out_shape=jax.ShapeDtypeStruct(own.shape, own.dtype),
        grid_spec=pltpu.PrefetchScalarGridSpec(
            num_scalar_prefetch=2,
            grid=(boxes,),
            in_specs=[
                pl.BlockSpec(memory_space=pl.ANY),
                pl.BlockSpec(memory_space=pl.ANY),
                block,
                full(far),
                full(near),
            ],
            out_specs=block,
            scratch_shapes=[
                pltpu.VMEM((total, width, orbs), own.dtype),
                pltpu.VMEM((width, orbs), F32),
                pltpu.SemaphoreType.DMA((total,)),
            ],
        ),
        compiler_params=pltpu.CompilerParams(vmem_limit_bytes=58 * 2**20),
    )(faces, count, own, come, part, far, near)


def shards(
    orbitals,
    exchange_values,
    local_values,
    coupling,
    to_values_mat,
    to_coeffs_mat,
    laplace_blocks,
    box_counts,
    kept_mask,
    send_list,
    neighbour_pos,
):
    k = to_values_mat.shape[0]
    fields = orbitals.transpose(1, 2, 0)
    exchange_fields = exchange_values.transpose(1, 2, 0)
    outgoing = pack(send_list[0], fields)
    incoming = lax.all_to_all(outgoing, "box", split_axis=0, concat_axis=0, tiled=True)

    apply = functools.partial(jnp.einsum, "ij,bjn->bin", preferred_element_type=F32)
    eye1, eye2 = jnp.eye(k, dtype=F32), jnp.eye(k * k, dtype=F32)
    cube = lambda m: jnp.kron(jnp.kron(m, m), m)
    high, low = split(cube(to_values_mat))
    values = apply(high, fields) + apply(low, fields)
    kept = (kept_mask > 0)[:, None, None]
    products = jnp.where(kept, exchange_fields.astype(F32) * values, 0.0).astype(BF16)
    gathered = lax.all_gather(products, "orb", axis=2, tiled=True)
    exchange = jnp.einsum("bcj,ij->bci", gathered, coupling, preferred_element_type=F32)
    weighted = local_values[:, :, None] * values - exchange
    high, low = split(cube(to_coeffs_mat))
    whigh = lax.reduce_precision(weighted, 8, 7)
    wlow = (weighted - whigh).astype(BF16)
    whigh = whigh.astype(BF16)
    part = apply(high, whigh) + apply(high, wlow) + apply(low, whigh)

    half = -0.5 * laplace_blocks
    own = half[0]
    center = (
        jnp.kron(own, eye2) + jnp.kron(jnp.kron(eye1, own), eye1) + jnp.kron(eye2, own)
    )
    high, low = split(center)
    part = part + apply(high, fields) + apply(low, fields)

    pair = jnp.eye(2, dtype=F32)
    far = jnp.stack([jnp.stack(split(jnp.kron(half[1 + s], eye2))) for s in range(2)])
    near = jnp.stack(
        [
            jnp.stack(split(jnp.kron(pair, m)))
            for m in (
                jnp.kron(half[1], eye1),
                jnp.kron(half[2], eye1),
                jnp.kron(eye1, half[1]),
                jnp.kron(eye1, half[2]),
            )
        ]
    )
    out = apply_faces(neighbour_pos, box_counts, fields, incoming, part, far, near)
    return out.transpose(2, 0, 1)


def solution(mesh):
    return jax.shard_map(
        shards,
        mesh=mesh,
        in_specs=(
            P("orb", "box", None),
            P("orb", "box", None),
            P("box", None),
            P("orb", None),
            P(),
            P(),
            P(),
            P("box"),
            P("box"),
            P("box", None),
            P(None, "box"),
        ),
        out_specs=P("orb", "box", None),
        check_vma=False,
    )
```

```python
import functools

import jax
import jax.numpy as jnp
from jax import lax
from jax.experimental import pallas as pl
from jax.experimental.pallas import tpu as pltpu
from jax.sharding import PartitionSpec as P

F32, BF16 = jnp.float32, jnp.bfloat16


def split(matrix):
    high = lax.reduce_precision(matrix, 8, 7)
    return high.astype(BF16), (matrix - high).astype(BF16)


def pack_kernel(slots, pool, out):
    out[...] = pool[...]


def pack(slots, pool):
    count = slots.shape[0]
    block = (1,) + pool.shape[1:]
    return pl.pallas_call(
        pack_kernel,
        out_shape=jax.ShapeDtypeStruct((count,) + pool.shape[1:], pool.dtype),
        grid_spec=pltpu.PrefetchScalarGridSpec(
            num_scalar_prefetch=1,
            grid=(count,),
            in_specs=[pl.BlockSpec(block, lambda p, at: (at[p], 0, 0))],
            out_specs=pl.BlockSpec(block, lambda p, at: (p, 0, 0)),
        ),
    )(slots, pool)


def spread(matrix, which):
    k = matrix.shape[0]
    width = k**3
    step = k ** (2 - which)
    flat = lax.broadcasted_iota(jnp.int32, (width, k), 0)
    pick = (flat // step % k == lax.broadcasted_iota(jnp.int32, (width, k), 1)).astype(F32)
    high = lax.Precision.HIGHEST
    return jnp.dot(jnp.dot(pick, matrix, precision=high), pick.T, precision=high)


def agree(k, which):
    flat = jnp.arange(k**3, dtype=jnp.int32)
    step = k ** (2 - which)
    rest = flat - flat // step % k * step
    return rest[:, None] == rest[None, :]


def alone(matrix, which):
    return jnp.where(agree(matrix.shape[0], which), spread(matrix, which), 0.0)


def faces_kernel(faces, count, own, come, part, far, near, out, pool, acc, sems):
    box_dev = own.shape[0]
    total = box_dev + come.shape[0]
    g = pl.program_id(0)

    def copy(n, ref, at):
        return pltpu.make_async_copy(ref.at[n], pool.at[at + n], sems.at[at + n])

    @pl.when(g == 0)
    def _():
        @pl.loop(0, box_dev)
        def _(n):
            copy(n, own, 0).start()

        @pl.loop(0, total - box_dev)
        def _(n):
            copy(n, come, box_dev).start()

        @pl.loop(0, box_dev)
        def _(n):
            copy(n, own, 0).wait()

        @pl.loop(0, total - box_dev)
        def _(n):
            copy(n, come, box_dev).wait()

    @pl.when(g >= count[0])
    def _():
        out[...] = jnp.zeros_like(out)

    @pl.when(g < count[0])
    def _():
        acc[...] = part[0]
        for f in range(6):
            at = faces[f, g]

            @pl.when(at >= 0)
            def _(f=f, at=at):
                x = pool[jnp.maximum(at, 0)]
                if f < 2:
                    acc[...] += jnp.dot(far[f, 0], x, preferred_element_type=F32) + jnp.dot(
                        far[f, 1], x, preferred_element_type=F32
                    )
                else:
                    size = near.shape[-1]
                    for j in range(x.shape[0] // size):
                        rows = pl.ds(j * size, size)
                        y = x[j * size : (j + 1) * size]
                        acc[rows, :] += jnp.dot(
                            near[f - 2, 0], y, preferred_element_type=F32
                        ) + jnp.dot(near[f - 2, 1], y, preferred_element_type=F32)

        out[0] = acc[...].astype(out.dtype)


def apply_faces(faces, count, own, come, part, far, near):
    boxes, width, orbs = own.shape
    total = boxes + come.shape[0]
    full = lambda a: pl.BlockSpec(a.shape, lambda g, *_: (0,) * a.ndim)
    block = pl.BlockSpec((1, width, orbs), lambda g, *_: (g, 0, 0))
    return pl.pallas_call(
        faces_kernel,
        out_shape=jax.ShapeDtypeStruct(own.shape, own.dtype),
        grid_spec=pltpu.PrefetchScalarGridSpec(
            num_scalar_prefetch=2,
            grid=(boxes,),
            in_specs=[
                pl.BlockSpec(memory_space=pl.ANY),
                pl.BlockSpec(memory_space=pl.ANY),
                block,
                full(far),
                full(near),
            ],
            out_specs=block,
            scratch_shapes=[
                pltpu.VMEM((total, width, orbs), own.dtype),
                pltpu.VMEM((width, orbs), F32),
                pltpu.SemaphoreType.DMA((total,)),
            ],
        ),
        compiler_params=pltpu.CompilerParams(vmem_limit_bytes=58 * 2**20),
    )(faces, count, own, come, part, far, near)


def shards(
    orbitals,
    exchange_values,
    local_values,
    coupling,
    to_values_mat,
    to_coeffs_mat,
    laplace_blocks,
    box_counts,
    kept_mask,
    send_list,
    neighbour_pos,
):
    k = to_values_mat.shape[0]
    fields = orbitals.transpose(1, 2, 0)
    exchange_fields = exchange_values.transpose(1, 2, 0)
    outgoing = pack(jnp.maximum(send_list[0], 0), fields)
    incoming = lax.all_to_all(outgoing, "box", split_axis=0, concat_axis=0, tiled=True)

    apply = functools.partial(jnp.einsum, "ij,bjn->bin", preferred_element_type=F32)
    cube = lambda m: spread(m, 0) * spread(m, 1) * spread(m, 2)
    high, low = split(cube(to_values_mat))
    values = apply(high, fields) + apply(low, fields)
    kept = (kept_mask > 0)[:, None, None]
    products = jnp.where(kept, exchange_fields.astype(F32) * values, 0.0).astype(BF16)
    gathered = lax.all_gather(products, "orb", axis=2, tiled=True)
    exchange = jnp.einsum("bcj,ij->bci", gathered, coupling, preferred_element_type=F32)
    weighted = local_values[:, :, None] * values - exchange
    high, low = split(cube(to_coeffs_mat))
    whigh = lax.reduce_precision(weighted, 8, 7)
    wlow = (weighted - whigh).astype(BF16)
    whigh = whigh.astype(BF16)
    part = apply(high, whigh) + apply(high, wlow) + apply(low, whigh)

    half = -0.5 * laplace_blocks
    center = alone(half[0], 0) + alone(half[0], 1) + alone(half[0], 2)
    high, low = split(center)
    part = part + apply(high, fields) + apply(low, fields)

    far = jnp.stack([jnp.stack(split(alone(half[1 + s], 0))) for s in range(2)])
    two = 2 * k * k
    near = jnp.stack(
        [
            jnp.stack(split(alone(half[1 + s], d)[:two, :two]))
            for d in (1, 2)
            for s in range(2)
        ]
    )
    out = apply_faces(neighbour_pos, box_counts, fields, incoming, part, far, near)
    return out.transpose(2, 0, 1)


def solution(mesh):
    return jax.shard_map(
        shards,
        mesh=mesh,
        in_specs=(
            P("orb", "box", None),
            P("orb", "box", None),
            P("box", None),
            P("orb", None),
            P(),
            P(),
            P(),
            P("box"),
            P("box"),
            P("box", None),
            P(None, "box"),
        ),
        out_specs=P("orb", "box", None),
        check_vma=False,
    )
```
